32 devices in a mesh: gx: 8 (over y, x, core), gy: 4 (over z).
Axes of the slice: x: 2, y: 2, z: 4, core: 2. Of those that a mesh axis runs over, the one named last changes fastest.
Arguments:
- subspace: float32 [16384, 256], P(('gx', 'gy')), may hold values from -15 to 15
- diag_blocks: float32 [32, 512, 512], P(('gx', 'gy')), may hold values from -0.25 to 0.25
- onsite: float32 [16384], P(('gx', 'gy')), may hold values from 0.5 to 4
- coupling: float32 [2, 32, 12, 128, 128], P(None, ('gx', 'gy')), may hold values from -0.1875 to 0.1875
- tile_rows: int32 [2, 32, 12], P(None, ('gx', 'gy')), may hold values from 0 to 3
- tile_cols: int32 [2, 32, 12], P(None, ('gx', 'gy')), may hold values from 0 to 3
- partner: int32 [2, 32], replicated, may hold values from 0 to 31, as said below
Outputs:
- basis: float32 [16384, 256], P(('gx', 'gy'))
- gram_scaled: float32 [256, 256], replicated
The draws below stay inside these ranges and needn't reach their ends.
Inputs may be any that keep to these rules, and one draw needn't show every extreme that they name: For each colour c there is one m_c, 1 to 31, with partner[c, i] = i XOR m_c for every device i; the two colours' m differ.
All inputs are finite; a program needn't handle non-finite values.
Results may differ from the reference program's by a relative error of at most 0.0003.
Values sent between devices are 32-bit elements; how exact they have to be, the bound alone decides.
A program may use at most 64 MiB of HBM per device.

```python
import math
import jax
import jax.numpy as jnp
from jax import lax

STATES = 256
TILE = 128
ROWS_DEV = 512
TILES = 12
COLOURS = 2
NS_ITERS = 12
BLOCKS = 4
NROWS = 16384
N_GX = 8
N_GY = 4


def draw_partner(key, part):
    devices = N_GX * N_GY
    lead_key, tail_key = jax.random.split(jax.random.fold_in(key, 11))
    lead_mask = jax.random.randint(lead_key, (), 1, devices, dtype=jnp.int32)
    offset = jax.random.randint(tail_key, (), 1, devices - 1, dtype=jnp.int32)
    tail_mask = (lead_mask - 1 + offset) % (devices - 1) + 1
    partner_masks = jnp.stack([lead_mask, tail_mask]).astype(jnp.int32)
    device_ids = jnp.arange(devices, dtype=jnp.int32)
    return jnp.bitwise_xor(device_ids[None, :], partner_masks[:, None]).astype(jnp.int32)


def draw_subspace(key, part):
    column_key, base_key = jax.random.split(jax.random.fold_in(key, 23), 2)
    column_scale = jnp.exp(jax.random.uniform(column_key, (STATES,), jnp.float32, math.log(0.3), math.log(3.0)))
    base = jnp.clip(jax.random.normal(base_key, (NROWS, STATES), jnp.float32), -5.0, 5.0)
    return (base * column_scale[None, :]).astype(jnp.float32)


def plant(values, own_key, low, largest):
    shape = values.shape
    place = [jax.random.randint(jax.random.fold_in(own_key, axis), (), 0, shape[axis]) for axis in range(len(shape))]
    values = values.at[tuple(place)].set(low)
    longest = shape.index(max(shape))
    place[longest] = (place[longest] + 1) % shape[longest]
    return values.at[tuple(place)].set(largest)


def block_scale(own_key, extent, shards, low, high):
    level = 1.0
    for position, parts in shards:
        heights = jax.random.uniform(jax.random.fold_in(jax.random.fold_in(own_key, 6), position), (parts,), jnp.float32, low / len(shards), high / len(shards))
        level = level * jnp.repeat(jnp.exp(heights), extent[position] // parts).reshape((-1,) + (1,) * (len(extent) - 1 - position))
    return level


def centred(stream_key, dims, scale, most, cuts=(), kind=jnp.bfloat16):
    values = scale * jax.random.normal(stream_key, dims, jnp.float32)
    if cuts:
        values = values * block_scale(stream_key, dims, cuts, -0.22, 0.18)
    return jnp.clip(values, -most, most).astype(kind)


def setup_inputs(seed: int = 0) -> dict:
    seeds = jax.random.split(jax.random.key(seed), 8)
    subspace = draw_subspace(jax.random.fold_in(seeds[7], 71), 0)
    diag_blocks = centred(seeds[1], (N_GX * N_GY, ROWS_DEV, ROWS_DEV), ROWS_DEV ** -0.5, 0.25, ((0, 32),), jnp.float32)
    onsite = jnp.clip(jnp.exp(math.log(4.0) - 2.0794415 * jax.random.uniform(seeds[2], (NROWS,), jnp.float32) ** block_scale(seeds[2], (NROWS,), ((0, 32),), -0.2, 0.2)), 0.5, 4.0)
    coupling = centred(seeds[3], (COLOURS, N_GX * N_GY, TILES, TILE, TILE), (TILE * 8) ** -0.5, 0.1875, ((1, 32),), jnp.float32)
    tile_rows = plant(jax.random.randint(seeds[4], (COLOURS, N_GX * N_GY, TILES), 0, BLOCKS), jax.random.fold_in(seeds[4], 1), 0, BLOCKS - 1).astype(jnp.int32)
    tile_cols = plant(jax.random.randint(seeds[5], (COLOURS, N_GX * N_GY, TILES), 0, BLOCKS), jax.random.fold_in(seeds[5], 1), 0, BLOCKS - 1).astype(jnp.int32)
    partner = draw_partner(jax.random.fold_in(seeds[7], 71), 0)
    return dict(subspace=subspace, diag_blocks=diag_blocks, onsite=onsite, coupling=coupling, tile_rows=tile_rows, tile_cols=tile_cols, partner=partner)


def apply_tiles(coupling_part, targets, picks, source, transposed):
    picked = source[picks]
    if transposed:
        products = jnp.einsum('kji,kjm->kim', coupling_part, picked, precision=lax.Precision.HIGHEST)
    else:
        products = jnp.einsum('kij,kjm->kim', coupling_part, picked, precision=lax.Precision.HIGHEST)
    placing = (targets[None, :] == jnp.arange(source.shape[0], dtype=jnp.int32)[:, None]).astype(jnp.float32)
    return jnp.einsum('bk,kim->bim', placing, products, precision=lax.Precision.HIGHEST)

def apply_hamiltonian(vectors, diag_blocks, onsite, coupling, tile_rows, tile_cols, partner):
    devices = N_GX * N_GY
    all_blocks = vectors.reshape(devices, BLOCKS, TILE, STATES)
    onsite_rows = onsite.reshape(devices, ROWS_DEV)

    def one_device(index):
        own_flat = all_blocks[index].reshape(ROWS_DEV, STATES)
        result = jnp.dot(diag_blocks[index], own_flat, precision=lax.Precision.HIGHEST, preferred_element_type=jnp.float32)
        result = result + onsite_rows[index][:, None] * own_flat
        for colour in range(COLOURS):
            mate = partner[colour, index]
            source = all_blocks[mate]
            forward = apply_tiles(coupling[colour, index], tile_rows[colour, index], tile_cols[colour, index], source, False)
            backward = apply_tiles(coupling[colour, mate], tile_cols[colour, mate], tile_rows[colour, mate], source, True)
            result = result + (forward + backward).reshape(ROWS_DEV, STATES)
        return result
    return lax.map(one_device, jnp.arange(devices, dtype=jnp.int32)).reshape(devices * ROWS_DEV, STATES)

def reference(subspace, diag_blocks, onsite, coupling, tile_rows, tile_cols, partner):

    def hamiltonian(vectors):
        return apply_hamiltonian(vectors, diag_blocks, onsite, coupling, tile_rows, tile_cols, partner)
    first = (hamiltonian(subspace) - 2.0 * subspace) / 4.0
    filtered = (hamiltonian(first) - 2.0 * first) / 2.0 - subspace
    gram_sum = jnp.dot(filtered.T, filtered, precision=lax.Precision.HIGHEST, preferred_element_type=jnp.float32)
    total_diag = jnp.trace(gram_sum)
    identity = jnp.eye(STATES, dtype=jnp.float32)
    iterate = gram_sum / total_diag
    inverse = identity
    for turn_index in range(NS_ITERS):
        factor = 1.5 * identity - 0.5 * jnp.dot(inverse, iterate, precision=lax.Precision.HIGHEST)
        iterate, inverse = (jnp.dot(iterate, factor, precision=lax.Precision.HIGHEST), jnp.dot(factor, inverse, precision=lax.Precision.HIGHEST))
    basis = jnp.dot(filtered, inverse, precision=lax.Precision.HIGHEST) * (jnp.sqrt(jnp.float32(NROWS)) / jnp.sqrt(total_diag))
    return (basis, gram_sum / NROWS)
```

```python
import functools

import jax
import jax.numpy as jnp
from jax import lax
from jax.experimental import pallas as pl
from jax.experimental.pallas import tpu as pltpu
from jax.sharding import PartitionSpec as P

NS_ITERS = 12
MESH = pl.DeviceIdType.MESH
VMEM_BYTES = 48 * 1024 * 1024


def split(values):
    high = values.astype(jnp.bfloat16)
    low = (values - high.astype(jnp.float32)).astype(jnp.bfloat16)
    return high, low


def dot3(left, right, contract=((1,), (0,))):
    def one(a, b):
        return lax.dot_general(a, b, (contract, ((), ())), preferred_element_type=jnp.float32)

    return one(left[0], right[0]) + (one(left[0], right[1]) + one(left[1], right[0]))


def exchange(masks, payload_of):
    devices = lax.axis_size("gx") * lax.axis_size("gy")

    def branch(bits):
        pairs = [(i, i ^ bits) for i in range(devices)]
        return lambda values: lax.ppermute(values, ("gx", "gy"), pairs)

    branches = [branch(bits) for bits in range(1, devices)]

    def one_colour(_, colour):
        return None, lax.switch(masks[colour] - 1, branches, payload_of(colour))

    return lax.scan(one_colour, None, jnp.arange(masks.shape[0]))[1]


def first_kernel(
    colours, own_rows, own_cols, far_rows, far_cols, own, diag, onsite, coupling, far,
    first, high, low, matrix,
):
    rows, states = own.shape
    size = coupling.shape[-1]
    tiles = coupling.shape[1]
    lead = rows * (states // size)
    matrix[:, :rows] = diag[...]
    matrix[:, rows:] = jnp.zeros((rows, colours * rows), jnp.float32)
    eye = lax.broadcasted_iota(jnp.int32, (size, size), 0) == lax.broadcasted_iota(
        jnp.int32, (size, size), 1
    )
    for block in range(rows // size):
        at = pl.ds(block * size, size)
        matrix[at, at] += jnp.where(eye, onsite[0:1, at] - 2.0, 0.0)

    def add(row, column, tile):
        down = pl.ds(pl.multiple_of(row * size, size), size)
        across = pl.ds(pl.multiple_of(column * size, size), size)
        matrix[down, across] += tile

    blocks = rows // size
    for colour in range(colours):

        @pl.loop(0, tiles)
        def _(k):
            add(
                own_rows[colour, k],
                own_cols[colour, k] + (colour + 1) * blocks,
                coupling[colour, k],
            )
            add(
                far_cols[colour, k],
                far_rows[colour, k] + (colour + 1) * blocks,
                far[colour, pl.ds(pl.multiple_of(lead + k * size, size), size), :].T,
            )

    sources = [split(own[...])]
    for colour in range(colours):
        pieces = [far[colour, pl.ds(at, rows), :] for at in range(0, lead, rows)]
        sources.append(split(jnp.concatenate(pieces, axis=1)))

    @pl.loop(0, blocks)
    def _(block):
        at = pl.ds(pl.multiple_of(block * size, size), size)
        total = jnp.zeros((size, own.shape[1]), jnp.float32)
        for place, source in enumerate(sources):
            across = pl.ds(place * rows, rows)
            left = split(matrix[at, across])
            high[at, across], low[at, across] = left
            total += dot3(left, source)
        first[at, :] = total * 0.25


def tail_kernel(colours, n_gx, n_gy, high, low, own, first, far, *refs):
    basis, gram_scaled = refs[:2]
    filtered, gram, gathered, arrive_x, arrive_y, send_x, recv_x, send_y, recv_y, send_g, recv_g = refs[2:]
    rows, states = own.shape
    me_x, me_y = lax.axis_index("gx"), lax.axis_index("gy")
    part = states // n_gx
    mine = pl.ds(pl.multiple_of(me_x * part, part), part)

    barrier = pltpu.get_barrier_semaphore()
    for k in range(1, n_gx):
        pl.semaphore_signal(
            barrier, inc=1, device_id=(lax.rem(me_x + k, n_gx), me_y), device_id_type=MESH
        )
    for k in range(1, n_gy):
        pl.semaphore_signal(
            barrier, inc=1, device_id=(me_x, lax.rem(me_y + k, n_gy)), device_id_type=MESH
        )

    size = 128
    sources = [split(first[...])] + [split(far[colour]) for colour in range(colours)]

    @pl.loop(0, rows // size)
    def _(block):
        at = pl.ds(pl.multiple_of(block * size, size), size)
        total = jnp.zeros((size, states), jnp.float32)
        for place, source in enumerate(sources):
            across = pl.ds(place * rows, rows)
            total += dot3((high[at, across], low[at, across]), source)
        filtered[at, :] = total * 0.5 - own[at, :]

    turned = split(filtered[...].T)
    upright = split(filtered[...])
    gram[...] = dot3(turned, upright)
    pl.semaphore_wait(barrier, n_gx - 1 + n_gy - 1)

    copies = []
    for k in range(1, n_gx):
        peer = lax.rem(me_x + k, n_gx)
        copies.append(
            pltpu.make_async_remote_copy(
                src_ref=gram.at[pl.ds(pl.multiple_of(peer * part, part), part), :],
                dst_ref=arrive_x.at[k],
                send_sem=send_x.at[k],
                recv_sem=recv_x.at[k],
                device_id=(peer, me_y),
                device_id_type=MESH,
            )
        )
        copies[-1].start()
    share = gram[mine, :]
    for k, copy in enumerate(copies, 1):
        copy.wait()
        share += arrive_x[k]
    arrive_y[me_y] = share

    copies = []
    for k in range(1, n_gy):
        copies.append(
            pltpu.make_async_remote_copy(
                src_ref=arrive_y.at[me_y],
                dst_ref=arrive_y.at[me_y],
                send_sem=send_y.at[k],
                recv_sem=recv_y.at[k],
                device_id=(me_x, lax.rem(me_y + k, n_gy)),
                device_id_type=MESH,
            )
        )
        copies[-1].start()
    for copy in copies:
        copy.wait()
    share = arrive_y[0]
    for k in range(1, n_gy):
        share += arrive_y[k]
    gathered[mine, :] = share

    copies = []
    for k in range(1, n_gx):
        copies.append(
            pltpu.make_async_remote_copy(
                src_ref=gathered.at[mine, :],
                dst_ref=gathered.at[mine, :],
                send_sem=send_g.at[k],
                recv_sem=recv_g.at[k],
                device_id=(lax.rem(me_x + k, n_gx), me_y),
                device_id_type=MESH,
            )
        )
        copies[-1].start()
    for copy in copies:
        copy.wait()

    order = float(rows * n_gx * n_gy)
    summed = gathered[...]
    gram_scaled[...] = summed * (1.0 / order)
    eye = lax.broadcasted_iota(jnp.int32, (states, states), 0) == lax.broadcasted_iota(
        jnp.int32, (states, states), 1
    )
    total = jnp.sum(jnp.where(eye, summed, 0.0), keepdims=True)

    def factor_of(product):
        return jnp.where(eye, 1.5, 0.0) - 0.5 * product

    iterate = summed / total
    factor = factor_of(iterate)
    iterate = dot3(split(iterate), split(factor))
    inverse = factor

    def turn(_, state):
        iterate, inverse = state
        iterate_parts, inverse_parts = split(iterate), split(inverse)
        factor = split(factor_of(dot3(inverse_parts, iterate_parts)))
        return dot3(iterate_parts, factor), dot3(factor, inverse_parts)

    iterate, inverse = lax.fori_loop(1, NS_ITERS, turn, (iterate, inverse))
    scale = jnp.sqrt(jnp.full((1, 1), order, jnp.float32)) / jnp.sqrt(total)
    basis[...] = dot3(upright, split(inverse)) * scale


def on_device(subspace, diag_blocks, onsite, coupling, tile_rows, tile_cols, partner):
    colours = partner.shape[0]
    rows, states = subspace.shape
    n_gx, n_gy = lax.axis_size("gx"), lax.axis_size("gy")
    masks = partner[:, 0]
    tiles, size = coupling.shape[2], coupling.shape[3]
    own_coupling = coupling.reshape(colours, tiles, size, size)
    own_rows = tile_rows.reshape(colours, tiles)
    own_cols = tile_cols.reshape(colours, tiles)
    places = jnp.stack([own_rows, own_cols], axis=1).astype(jnp.float32)
    places = jnp.pad(places, ((0, 0), (0, 8 - 2), (0, size - tiles)))
    pieces = [subspace[:, at : at + size] for at in range(0, states, size)]
    packed = jnp.stack(
        [
            jnp.concatenate([*pieces, own_coupling[c].reshape(tiles * size, size), places[c]])
            for c in range(colours)
        ]
    )
    far = exchange(masks, lambda colour: lax.dynamic_index_in_dim(packed, colour, 0, False))
    far_places = far[:, -8:-6, :tiles].astype(jnp.int32)
    vmem = pl.BlockSpec(memory_space=pltpu.VMEM)
    smem = pl.BlockSpec(memory_space=pltpu.SMEM)
    wide = (rows, (colours + 1) * rows)
    flops = 6 * rows * wide[1] * states
    first, high, low = pl.pallas_call(
        functools.partial(first_kernel, colours),
        out_shape=(
            jax.ShapeDtypeStruct((rows, states), jnp.float32),
            jax.ShapeDtypeStruct(wide, jnp.bfloat16),
            jax.ShapeDtypeStruct(wide, jnp.bfloat16),
        ),
        in_specs=[smem] * 4 + [vmem] * 5,
        out_specs=(vmem, vmem, vmem),
        scratch_shapes=[pltpu.VMEM(wide, jnp.float32)],
        compiler_params=pltpu.CompilerParams(vmem_limit_bytes=VMEM_BYTES),
        cost_estimate=pl.CostEstimate(flops=flops, bytes_accessed=2**23, transcendentals=0),
        name="first",
    )(
        own_rows,
        own_cols,
        far_places[:, 0],
        far_places[:, 1],
        subspace,
        diag_blocks.reshape(rows, rows),
        onsite.reshape(1, rows),
        own_coupling,
        far,
    )

    far_first = exchange(masks, lambda colour: first)
    part = states // n_gx
    dma = pltpu.SemaphoreType.DMA
    return pl.pallas_call(
        functools.partial(tail_kernel, colours, n_gx, n_gy),
        out_shape=(
            jax.ShapeDtypeStruct((rows, states), jnp.float32),
            jax.ShapeDtypeStruct((states, states), jnp.float32),
        ),
        in_specs=[vmem] * 5,
        out_specs=(vmem, vmem),
        scratch_shapes=[
            pltpu.VMEM((rows, states), jnp.float32),
            pltpu.VMEM((states, states), jnp.float32),
            pltpu.VMEM((states, states), jnp.float32),
            pltpu.VMEM((n_gx, part, states), jnp.float32),
            pltpu.VMEM((n_gy, part, states), jnp.float32),
            dma((n_gx,)),
            dma((n_gx,)),
            dma((n_gy,)),
            dma((n_gy,)),
            dma((n_gx,)),
            dma((n_gx,)),
        ],
        compiler_params=pltpu.CompilerParams(
            vmem_limit_bytes=VMEM_BYTES, collective_id=0, has_side_effects=True
        ),
        cost_estimate=pl.CostEstimate(flops=2 * flops, bytes_accessed=2**23, transcendentals=0),
        name="tail",
    )(high, low, subspace, first, far_first)


def solution(mesh):
    placed = (
        P(("gx", "gy"), None),
        P(("gx", "gy"), None, None),
        P(("gx", "gy")),
        P(None, ("gx", "gy"), None, None, None),
        P(None, ("gx", "gy"), None),
        P(None, ("gx", "gy"), None),
        P(),
    )
    return jax.shard_map(
        on_device,
        mesh=mesh,
        in_specs=placed,
        out_specs=(P(("gx", "gy"), None), P()),
        check_vma=False,
    )
```

```python
import functools

import jax
import jax.numpy as jnp
from jax import lax
from jax.experimental import pallas as pl
from jax.experimental.pallas import tpu as pltpu
from jax.sharding import PartitionSpec as P

NS_ITERS = 12
MESH = pl.DeviceIdType.MESH
VMEM_BYTES = 48 * 1024 * 1024


def split(values):
    high = values.astype(jnp.bfloat16)
    low = (values - high.astype(jnp.float32)).astype(jnp.bfloat16)
    return high, low


def dot3(left, right):
    (left_high, left_low), (right_high, right_low) = left, right
    return jnp.dot(
        jnp.concatenate([left_high, left_high, left_low], axis=1),
        jnp.concatenate([right_high, right_low, right_high], axis=0),
        preferred_element_type=jnp.float32,
    )


def wide_dot(high, low, parts_high, parts_low):
    def one(left, right):
        return jnp.dot(left[...], right[...], preferred_element_type=jnp.float32)

    return one(high, parts_high) + (one(high, parts_low) + one(low, parts_high))


def place_parts(sources, parts_high, parts_low):
    for place, source in enumerate(sources):
        at = pl.ds(place * source.shape[0], source.shape[0])
        parts_high[at, :], parts_low[at, :] = split(source)


def exchange(mask, payload):
    devices = lax.axis_size("gx") * lax.axis_size("gy")

    def branch(bits):
        pairs = [(i, i ^ bits) for i in range(devices)]
        return lambda values: lax.ppermute(values, ("gx", "gy"), pairs)

    return lax.switch(mask - 1, [branch(bits) for bits in range(1, devices)], payload)


def first_kernel(
    colours, own_rows, own_cols, far_rows, far_cols, own, diag, onsite, coupling, *refs
):
    far, (first, high, low, matrix, parts_high, parts_low) = refs[:colours], refs[colours:]
    rows, states = own.shape
    size = coupling.shape[-1]
    tiles = coupling.shape[1]
    lead = rows * (states // size)
    matrix[:, :rows] = diag[...]
    matrix[:, rows:] = jnp.zeros((rows, colours * rows), jnp.float32)
    eye = lax.broadcasted_iota(jnp.int32, (size, size), 0) == lax.broadcasted_iota(
        jnp.int32, (size, size), 1
    )
    for block in range(rows // size):
        at = pl.ds(block * size, size)
        matrix[at, at] += jnp.where(eye, onsite[0:1, at] - 2.0, 0.0)

    def add(row, column, tile):
        down = pl.ds(pl.multiple_of(row * size, size), size)
        across = pl.ds(pl.multiple_of(column * size, size), size)
        matrix[down, across] += tile

    blocks = rows // size
    for colour in range(colours):

        @pl.loop(0, tiles)
        def _(k):
            add(
                own_rows[colour, k],
                own_cols[colour, k] + (colour + 1) * blocks,
                coupling[colour, k],
            )
            add(
                far_cols[colour, k],
                far_rows[colour, k] + (colour + 1) * blocks,
                far[colour][pl.ds(pl.multiple_of(lead + k * size, size), size), :].T,
            )

    sources = [own[...]]
    for colour in range(colours):
        pieces = [far[colour][pl.ds(at, rows), :] for at in range(0, lead, rows)]
        sources.append(jnp.concatenate(pieces, axis=1))
    place_parts(sources, parts_high, parts_low)

    @pl.loop(0, blocks)
    def _(block):
        at = pl.ds(pl.multiple_of(block * size, size), size)
        high[at, :], low[at, :] = split(matrix[at, :])

    first[...] = wide_dot(high, low, parts_high, parts_low) * 0.25


def tail_kernel(colours, n_gx, n_gy, high, low, own, first, *refs):
    far = refs[:colours]
    basis, gram_scaled = refs[colours : colours + 2]
    parts_high, parts_low, gram, gathered, arrive_x, arrive_y, send_x, recv_x, send_y, recv_y, send_g, recv_g = refs[
        colours + 2 :
    ]
    rows, states = own.shape
    me_x, me_y = lax.axis_index("gx"), lax.axis_index("gy")
    part = states // n_gx
    mine = pl.ds(pl.multiple_of(me_x * part, part), part)

    barrier = pltpu.get_barrier_semaphore()
    for k in range(1, n_gx):
        pl.semaphore_signal(
            barrier, inc=1, device_id=(lax.rem(me_x + k, n_gx), me_y), device_id_type=MESH
        )
    for k in range(1, n_gy):
        pl.semaphore_signal(
            barrier, inc=1, device_id=(me_x, lax.rem(me_y + k, n_gy)), device_id_type=MESH
        )

    place_parts([ref[...] for ref in (first, *far)], parts_high, parts_low)
    filtered = wide_dot(high, low, parts_high, parts_low) * 0.5 - own[...]
    turned, upright = split(filtered.T), split(filtered)
    gram[...] = dot3(turned, upright)
    pl.semaphore_wait(barrier, n_gx - 1 + n_gy - 1)

    copies = []
    for k in range(1, n_gx):
        peer = lax.rem(me_x + k, n_gx)
        copies.append(
            pltpu.make_async_remote_copy(
                src_ref=gram.at[pl.ds(pl.multiple_of(peer * part, part), part), :],
                dst_ref=arrive_x.at[k],
                send_sem=send_x.at[k],
                recv_sem=recv_x.at[k],
                device_id=(peer, me_y),
                device_id_type=MESH,
            )
        )
        copies[-1].start()
    share = gram[mine, :]
    for k, copy in enumerate(copies, 1):
        copy.wait()
        share += arrive_x[k]
    arrive_y[me_y] = share

    copies = []
    for k in range(1, n_gy):
        copies.append(
            pltpu.make_async_remote_copy(
                src_ref=arrive_y.at[me_y],
                dst_ref=arrive_y.at[me_y],
                send_sem=send_y.at[k],
                recv_sem=recv_y.at[k],
                device_id=(me_x, lax.rem(me_y + k, n_gy)),
                device_id_type=MESH,
            )
        )
        copies[-1].start()
    for copy in copies:
        copy.wait()
    share = arrive_y[0]
    for k in range(1, n_gy):
        share += arrive_y[k]
    gathered[mine, :] = share

    copies = []
    for k in range(1, n_gx):
        copies.append(
            pltpu.make_async_remote_copy(
                src_ref=gathered.at[mine, :],
                dst_ref=gathered.at[mine, :],
                send_sem=send_g.at[k],
                recv_sem=recv_g.at[k],
                device_id=(lax.rem(me_x + k, n_gx), me_y),
                device_id_type=MESH,
            )
        )
        copies[-1].start()
    for copy in copies:
        copy.wait()

    order = float(rows * n_gx * n_gy)
    summed = gathered[...]
    gram_scaled[...] = summed * (1.0 / order)
    eye = lax.broadcasted_iota(jnp.int32, (states, states), 0) == lax.broadcasted_iota(
        jnp.int32, (states, states), 1
    )
    total = jnp.sum(jnp.where(eye, summed, 0.0), keepdims=True)

    def factor_of(product):
        return jnp.where(eye, 1.5, 0.0) - 0.5 * product

    iterate = summed / total
    factor = factor_of(iterate)
    iterate = dot3(split(iterate), split(factor))
    inverse = factor

    def turn(_, state):
        iterate, inverse = state
        iterate_parts, inverse_parts = split(iterate), split(inverse)
        factor = split(factor_of(dot3(inverse_parts, iterate_parts)))
        return dot3(iterate_parts, factor), dot3(factor, inverse_parts)

    iterate, inverse = lax.fori_loop(1, NS_ITERS, turn, (iterate, inverse))
    scale = jnp.sqrt(jnp.full((1, 1), order, jnp.float32)) / jnp.sqrt(total)
    basis[...] = dot3(upright, split(inverse)) * scale


def on_device(subspace, diag_blocks, onsite, coupling, tile_rows, tile_cols, partner):
    colours = partner.shape[0]
    rows, states = subspace.shape
    n_gx, n_gy = lax.axis_size("gx"), lax.axis_size("gy")
    masks = [partner[colour, 0] for colour in range(colours)]
    tiles, size = coupling.shape[2], coupling.shape[3]
    own_coupling = coupling.reshape(colours, tiles, size, size)
    own_rows = tile_rows.reshape(colours, tiles)
    own_cols = tile_cols.reshape(colours, tiles)
    places = jnp.stack([own_rows, own_cols], axis=1).astype(jnp.float32)
    places = jnp.pad(places, ((0, 0), (0, 8 - 2), (0, size - tiles)))
    pieces = [subspace[:, at : at + size] for at in range(0, states, size)]
    packed = [
        jnp.concatenate([*pieces, own_coupling[c].reshape(tiles * size, size), places[c]])
        for c in range(colours)
    ]
    far = [exchange(masks[c], packed[c]) for c in range(colours)]
    far_places = jnp.stack([part[-8:-6, :tiles] for part in far]).astype(jnp.int32)
    vmem = pl.BlockSpec(memory_space=pltpu.VMEM)
    smem = pl.BlockSpec(memory_space=pltpu.SMEM)
    wide = (rows, (colours + 1) * rows)
    parts = [pltpu.VMEM((wide[1], states), jnp.bfloat16)] * 2
    flops = 6 * rows * wide[1] * states
    first, high, low = pl.pallas_call(
        functools.partial(first_kernel, colours),
        out_shape=(
            jax.ShapeDtypeStruct((rows, states), jnp.float32),
            jax.ShapeDtypeStruct(wide, jnp.bfloat16),
            jax.ShapeDtypeStruct(wide, jnp.bfloat16),
        ),
        in_specs=[smem] * 4 + [vmem] * (4 + colours),
        out_specs=(vmem, vmem, vmem),
        scratch_shapes=[pltpu.VMEM(wide, jnp.float32), *parts],
        compiler_params=pltpu.CompilerParams(vmem_limit_bytes=VMEM_BYTES),
        cost_estimate=pl.CostEstimate(flops=flops, bytes_accessed=2**23, transcendentals=0),
        name="first",
    )(
        own_rows,
        own_cols,
        far_places[:, 0],
        far_places[:, 1],
        subspace,
        diag_blocks.reshape(rows, rows),
        onsite.reshape(1, rows),
        own_coupling,
        *far,
    )

    far_first = [exchange(mask, first) for mask in masks]
    part = states // n_gx
    dma = pltpu.SemaphoreType.DMA
    return pl.pallas_call(
        functools.partial(tail_kernel, colours, n_gx, n_gy),
        out_shape=(
            jax.ShapeDtypeStruct((rows, states), jnp.float32),
            jax.ShapeDtypeStruct((states, states), jnp.float32),
        ),
        in_specs=[vmem] * (4 + colours),
        out_specs=(vmem, vmem),
        scratch_shapes=[
            *parts,
            pltpu.VMEM((states, states), jnp.float32),
            pltpu.VMEM((states, states), jnp.float32),
            pltpu.VMEM((n_gx, part, states), jnp.float32),
            pltpu.VMEM((n_gy, part, states), jnp.float32),
            dma((n_gx,)),
            dma((n_gx,)),
            dma((n_gy,)),
            dma((n_gy,)),
            dma((n_gx,)),
            dma((n_gx,)),
        ],
        compiler_params=pltpu.CompilerParams(
            vmem_limit_bytes=VMEM_BYTES, collective_id=0, has_side_effects=True
        ),
        cost_estimate=pl.CostEstimate(flops=2 * flops, bytes_accessed=2**23, transcendentals=0),
        name="tail",
    )(high, low, subspace, first, *far_first)


def solution(mesh):
    placed = (
        P(("gx", "gy"), None),
        P(("gx", "gy"), None, None),
        P(("gx", "gy")),
        P(None, ("gx", "gy"), None, None, None),
        P(None, ("gx", "gy"), None),
        P(None, ("gx", "gy"), None),
        P(),
    )
    return jax.shard_map(
        on_device,
        mesh=mesh,
        in_specs=placed,
        out_specs=(P(("gx", "gy"), None), P()),
        check_vma=False,
    )
```

```python
import functools

import jax
import jax.numpy as jnp
from jax import lax
from jax.experimental import pallas as pl
from jax.experimental.pallas import tpu as pltpu
from jax.sharding import PartitionSpec as P

NS_ITERS = 12
MESH = pl.DeviceIdType.MESH
VMEM_BYTES = 48 * 1024 * 1024


def split(values):
    high = values.astype(jnp.bfloat16)
    low = (values - high.astype(jnp.float32)).astype(jnp.bfloat16)
    return high, low


def dot3(left, right):
    (left_high, left_low), (right_high, right_low) = left, right
    return jnp.dot(
        jnp.concatenate([left_high, left_high, left_low], axis=1),
        jnp.concatenate([right_high, right_low, right_high], axis=0),
        preferred_element_type=jnp.float32,
    )


def wide_dot(high, low, parts_high, parts_low):
    def one(left, right):
        return jnp.dot(left[...], right[...], preferred_element_type=jnp.float32)

    return one(high, parts_high) + (one(high, parts_low) + one(low, parts_high))


def place_parts(sources, parts_high, parts_low):
    for place, source in enumerate(sources):
        at = pl.ds(place * source.shape[0], source.shape[0])
        parts_high[at, :], parts_low[at, :] = split(source)


def exchange(mask, payload):
    devices = lax.axis_size("gx") * lax.axis_size("gy")

    def branch(bits):
        pairs = [(i, i ^ bits) for i in range(devices)]
        return lambda values: lax.ppermute(values, ("gx", "gy"), pairs)

    return lax.switch(mask - 1, [branch(bits) for bits in range(1, devices)], payload)


def first_kernel(
    colours, own_rows, own_cols, far_rows, far_cols, own, diag, onsite, coupling, *refs
):
    far, (first, high, low, matrix, parts_high, parts_low) = refs[:colours], refs[colours:]
    rows, states = own.shape
    size = coupling.shape[-1]
    tiles = coupling.shape[1]
    lead = rows * (states // size)
    matrix[:, :rows] = diag[...]
    matrix[:, rows:] = jnp.zeros((rows, colours * rows), jnp.float32)
    eye = lax.broadcasted_iota(jnp.int32, (size, size), 0) == lax.broadcasted_iota(
        jnp.int32, (size, size), 1
    )
    for block in range(rows // size):
        at = pl.ds(block * size, size)
        matrix[at, at] += jnp.where(eye, onsite[0:1, at] - 2.0, 0.0)

    def add(row, column, tile):
        down = pl.ds(pl.multiple_of(row * size, size), size)
        across = pl.ds(pl.multiple_of(column * size, size), size)
        matrix[down, across] += tile

    blocks = rows // size
    for colour in range(colours):

        @pl.loop(0, tiles)
        def _(k):
            add(
                own_rows[colour, k],
                own_cols[colour, k] + (colour + 1) * blocks,
                coupling[colour, k],
            )
            add(
                far_cols[colour, k],
                far_rows[colour, k] + (colour + 1) * blocks,
                far[colour][pl.ds(pl.multiple_of(lead + k * size, size), size), :].T,
            )

    sources = [own[...]]
    for colour in range(colours):
        pieces = [far[colour][pl.ds(at, rows), :] for at in range(0, lead, rows)]
        sources.append(jnp.concatenate(pieces, axis=1))
    place_parts(sources, parts_high, parts_low)

    @pl.loop(0, blocks)
    def _(block):
        at = pl.ds(pl.multiple_of(block * size, size), size)
        high[at, :], low[at, :] = split(matrix[at, :])

    first[...] = wide_dot(high, low, parts_high, parts_low) * 0.25


def tail_kernel(colours, n_gx, n_gy, high, low, own, first, *refs):
    far = refs[:colours]
    basis, gram_scaled = refs[colours : colours + 2]
    parts_high, parts_low, gram, gathered, arrive_x, arrive_y, send_x, recv_x, send_y, recv_y, send_g, recv_g = refs[
        colours + 2 :
    ]
    rows, states = own.shape
    me_x, me_y = lax.axis_index("gx"), lax.axis_index("gy")
    part = states // n_gx
    mine = pl.ds(pl.multiple_of(me_x * part, part), part)

    barrier = pltpu.get_barrier_semaphore()
    for k in range(1, n_gx):
        pl.semaphore_signal(
            barrier, inc=1, device_id=(lax.rem(me_x + k, n_gx), me_y), device_id_type=MESH
        )
    for k in range(1, n_gy):
        pl.semaphore_signal(
            barrier, inc=1, device_id=(me_x, lax.rem(me_y + k, n_gy)), device_id_type=MESH
        )

    place_parts([ref[...] for ref in (first, *far)], parts_high, parts_low)
    filtered = wide_dot(high, low, parts_high, parts_low) * 0.5 - own[...]
    turned, upright = split(filtered.T), split(filtered)
    gram[...] = dot3(turned, upright)
    pl.semaphore_wait(barrier, n_gx - 1 + n_gy - 1)

    copies = []
    for k in range(1, n_gx):
        peer = lax.rem(me_x + k, n_gx)
        copies.append(
            pltpu.make_async_remote_copy(
                src_ref=gram.at[pl.ds(pl.multiple_of(peer * part, part), part), :],
                dst_ref=arrive_x.at[k],
                send_sem=send_x.at[k],
                recv_sem=recv_x.at[k],
                device_id=(peer, me_y),
                device_id_type=MESH,
            )
        )
        copies[-1].start()
    share = gram[mine, :]
    for k, copy in enumerate(copies, 1):
        copy.wait()
        share += arrive_x[k]
    arrive_y[me_y] = share

    copies = []
    for k in range(1, n_gy):
        copies.append(
            pltpu.make_async_remote_copy(
                src_ref=arrive_y.at[me_y],
                dst_ref=arrive_y.at[me_y],
                send_sem=send_y.at[k],
                recv_sem=recv_y.at[k],
                device_id=(me_x, lax.rem(me_y + k, n_gy)),
                device_id_type=MESH,
            )
        )
        copies[-1].start()
    for copy in copies:
        copy.wait()
    share = arrive_y[0]
    for k in range(1, n_gy):
        share += arrive_y[k]
    gathered[mine, :] = share

    copies = []
    for k in range(1, n_gx):
        copies.append(
            pltpu.make_async_remote_copy(
                src_ref=gathered.at[mine, :],
                dst_ref=gathered.at[mine, :],
                send_sem=send_g.at[k],
                recv_sem=recv_g.at[k],
                device_id=(lax.rem(me_x + k, n_gx), me_y),
                device_id_type=MESH,
            )
        )
        copies[-1].start()
    for copy in copies:
        copy.wait()

    order = float(rows * n_gx * n_gy)
    summed = gathered[...]
    gram_scaled[...] = summed * (1.0 / order)
    eye = lax.broadcasted_iota(jnp.int32, (states, states), 0) == lax.broadcasted_iota(
        jnp.int32, (states, states), 1
    )
    total = jnp.sum(jnp.where(eye, summed, 0.0), keepdims=True)

    def factor_of(product):
        return jnp.where(eye, 1.5, 0.0) - 0.5 * product

    iterate = summed / total
    factor = factor_of(iterate)
    iterate = dot3(split(iterate), split(factor))
    inverse = factor

    for turn in range(1, NS_ITERS):
        iterate_parts, inverse_parts = split(iterate), split(inverse)
        factor = split(factor_of(dot3(inverse_parts, iterate_parts)))
        inverse = dot3(factor, inverse_parts)
        if turn < NS_ITERS - 1:
            iterate = dot3(iterate_parts, factor)
    scale = jnp.sqrt(jnp.full((1, 1), order, jnp.float32)) / jnp.sqrt(total)
    basis[...] = dot3(upright, split(inverse)) * scale


def on_device(subspace, diag_blocks, onsite, coupling, tile_rows, tile_cols, partner):
    colours = partner.shape[0]
    rows, states = subspace.shape
    n_gx, n_gy = lax.axis_size("gx"), lax.axis_size("gy")
    masks = [partner[colour, 0] for colour in range(colours)]
    tiles, size = coupling.shape[2], coupling.shape[3]
    own_coupling = coupling.reshape(colours, tiles, size, size)
    own_rows = tile_rows.reshape(colours, tiles)
    own_cols = tile_cols.reshape(colours, tiles)
    places = jnp.stack([own_rows, own_cols], axis=1).astype(jnp.float32)
    places = jnp.pad(places, ((0, 0), (0, 8 - 2), (0, size - tiles)))
    pieces = [subspace[:, at : at + size] for at in range(0, states, size)]
    packed = [
        jnp.concatenate([*pieces, own_coupling[c].reshape(tiles * size, size), places[c]])
        for c in range(colours)
    ]
    far = [exchange(masks[c], packed[c]) for c in range(colours)]
    far_places = jnp.stack([part[-8:-6, :tiles] for part in far]).astype(jnp.int32)
    vmem = pl.BlockSpec(memory_space=pltpu.VMEM)
    smem = pl.BlockSpec(memory_space=pltpu.SMEM)
    wide = (rows, (colours + 1) * rows)
    parts = [pltpu.VMEM((wide[1], states), jnp.bfloat16)] * 2
    flops = 6 * rows * wide[1] * states
    first, high, low = pl.pallas_call(
        functools.partial(first_kernel, colours),
        out_shape=(
            jax.ShapeDtypeStruct((rows, states), jnp.float32),
            jax.ShapeDtypeStruct(wide, jnp.bfloat16),
            jax.ShapeDtypeStruct(wide, jnp.bfloat16),
        ),
        in_specs=[smem] * 4 + [vmem] * (4 + colours),
        out_specs=(vmem, vmem, vmem),
        scratch_shapes=[pltpu.VMEM(wide, jnp.float32), *parts],
        compiler_params=pltpu.CompilerParams(vmem_limit_bytes=VMEM_BYTES),
        cost_estimate=pl.CostEstimate(flops=flops, bytes_accessed=2**23, transcendentals=0),
        name="first",
    )(
        own_rows,
        own_cols,
        far_places[:, 0],
        far_places[:, 1],
        subspace,
        diag_blocks.reshape(rows, rows),
        onsite.reshape(1, rows),
        own_coupling,
        *far,
    )

    far_first = [exchange(mask, first) for mask in masks]
    part = states // n_gx
    dma = pltpu.SemaphoreType.DMA
    return pl.pallas_call(
        functools.partial(tail_kernel, colours, n_gx, n_gy),
        out_shape=(
            jax.ShapeDtypeStruct((rows, states), jnp.float32),
            jax.ShapeDtypeStruct((states, states), jnp.float32),
        ),
        in_specs=[vmem] * (4 + colours),
        out_specs=(vmem, vmem),
        scratch_shapes=[
            *parts,
            pltpu.VMEM((states, states), jnp.float32),
            pltpu.VMEM((states, states), jnp.float32),
            pltpu.VMEM((n_gx, part, states), jnp.float32),
            pltpu.VMEM((n_gy, part, states), jnp.float32),
            dma((n_gx,)),
            dma((n_gx,)),
            dma((n_gy,)),
            dma((n_gy,)),
            dma((n_gx,)),
            dma((n_gx,)),
        ],
        compiler_params=pltpu.CompilerParams(
            vmem_limit_bytes=VMEM_BYTES, collective_id=0, has_side_effects=True
        ),
        cost_estimate=pl.CostEstimate(flops=2 * flops, bytes_accessed=2**23, transcendentals=0),
        name="tail",
    )(high, low, subspace, first, *far_first)


def solution(mesh):
    placed = (
        P(("gx", "gy"), None),
        P(("gx", "gy"), None, None),
        P(("gx", "gy")),
        P(None, ("gx", "gy"), None, None, None),
        P(None, ("gx", "gy"), None),
        P(None, ("gx", "gy"), None),
        P(),
    )
    return jax.shard_map(
        on_device,
        mesh=mesh,
        in_specs=placed,
        out_specs=(P(("gx", "gy"), None), P()),
        check_vma=False,
    )
```
